32 devices in a mesh: dp: 4 (over y, x), ctx: 4 (over z), mp: 2 (over core).
Axes of the slice: x: 2, y: 2, z: 4, core: 2. Of those that a mesh axis runs over, the one named last changes fastest.
Arguments:
- tokens: bfloat16 [4096, 2304], P(('dp', 'ctx')), may hold values from -6 to 6
- cotangent: bfloat16 [4096, 2304], P(('dp', 'ctx')), may hold values from -6 to 6
- segments: int32 [4096], replicated, may hold values from 0 to 7, never falling along the last dimension, each value on 1 to 2048 neighbouring positions
- padding: int32 [4096], replicated, may hold values 0 or 1
- owners: int32 [7, 4], replicated, may hold values from 0 to 3, each once within a row
- gains: float32 [4, 2304], replicated, may hold values from 0.5 to 1.5
- gain_stats: float32 [4, 2304], replicated, may hold values from 4096 to 16384
- attention_input_master: float32 [2304, 4096], P('dp', ('ctx', 'mp')), may hold values from -0.125 to 0.125
- attn_out: float32 [2304, 2048], P('dp', ('ctx', 'mp')), may hold values from -0.5 to 0.5
- mlp_in: float32 [2304, 18432], P('dp', ('ctx', 'mp')), may hold values from -0.125 to 0.125
- mlp_out: float32 [2304, 9216], P('dp', ('ctx', 'mp')), may hold values from -0.0625 to 0.0625
- left_stats: float32 [4, 4, 2, 33, 576, 576], P('dp', 'ctx', 'mp'), may hold values from -104858 to 524288
- right_stats: float32 [4, 4, 2, 33, 128, 128], P('dp', 'ctx', 'mp'), may hold values from -471860 to 2359296
- left_roots: float32 [4, 4, 2, 33, 576, 576], P('dp', 'ctx', 'mp'), may hold values from -0.042044821 to 0.07357844
- right_roots: float32 [4, 4, 2, 33, 128, 128], P('dp', 'ctx', 'mp'), may hold values from -0.028867513 to 0.050518149
Outputs:
- block_out: bfloat16 [4096, 2304], P(('dp', 'ctx'))
- input_grad: float32 [4096, 2304], P(('dp', 'ctx'))
- grad_attn_in: float32 [2304, 4096], P('dp', ('ctx', 'mp'))
- grad_attn_out: float32 [2304, 2048], P('dp', ('ctx', 'mp'))
- grad_mlp_in: float32 [2304, 18432], P('dp', ('ctx', 'mp'))
- grad_mlp_out: float32 [2304, 9216], P('dp', ('ctx', 'mp'))
- new_attn_in: float32 [2304, 4096], P('dp', ('ctx', 'mp'))
- new_attn_out: float32 [2304, 2048], P('dp', ('ctx', 'mp'))
- new_mlp_in: float32 [2304, 18432], P('dp', ('ctx', 'mp'))
- new_mlp_out: float32 [2304, 9216], P('dp', ('ctx', 'mp'))
- new_left: float32 [4, 4, 2, 33, 576, 576], P('dp', 'ctx', 'mp')
- new_right: float32 [4, 4, 2, 33, 128, 128], P('dp', 'ctx', 'mp')
- gain_grad: float32 [4, 2304], replicated
- new_gain_stats: float32 [4, 2304], replicated
- new_gains: float32 [4, 2304], replicated
The draws below stay inside these ranges and needn't reach their ends.
Inputs may be any that keep to these rules, and one draw needn't show every extreme that they name: `segments`: never falling along the tokens; a segment holds 1 to 2048 tokens, one exactly that many. `owners`: each row is a permutation.
All inputs are finite; a program needn't handle non-finite values.
Results may differ from the reference program's by a relative error of at most 0.02.
Values may be sent and summed in bfloat16 or wider, within the bound.
No kernel may reach another device: no remote copies, remote signals or barrier semaphores. Data moves between devices by JAX's collectives and lax.ppermute only.
A program may use at most 896 MiB of HBM per device.

```python
import math
import jax
import jax.numpy as jnp
import numpy as np
from jax import lax

MODEL_WIDTH = 2304
HEAD_SIZE = 256
QUERY_HEADS = 8
KEY_VALUE_HEADS = 4
FF = 9216
TOK_DEV = 256
PACKED_TOKENS = 4096
WINDOW = 1024
SUBW = 128
TOKENS = 4096
DB = 576
NBLK = 33
N_DP = 4
N_CTX = 4
N_MP = 2


def diagonal_part(key, lead, size, low_end, high_end):
    unit = jax.random.uniform(key, lead + (size,), dtype=jnp.float32)
    values = low_end * jnp.exp(unit * math.log(high_end / low_end))
    identity = (jnp.arange(size)[:, None] == jnp.arange(size)[None, :]).astype(jnp.float32)
    return values[..., :, None] * identity


def off_part(noise, size, amount):
    symmetric = (noise + jnp.swapaxes(noise, -1, -2)) * (1.0 / math.sqrt(2.0))
    identity = (jnp.arange(size)[:, None] == jnp.arange(size)[None, :]).astype(jnp.float32)
    return symmetric * (1.0 - identity) * (amount / math.sqrt(size))


def square_draw(key, size, scale, low_end, high_end):
    first, second = jax.random.split(key)
    lead = (N_DP, N_CTX, N_MP, NBLK)
    noise = jax.random.truncated_normal(second, -4.0, 4.0, lead + (size, size), dtype=jnp.float32)
    return (scale * (diagonal_part(first, lead, size, low_end, high_end) + off_part(noise, size, 0.4))).astype(jnp.float32)


def draw_left_stats(key, part):
    key = jax.random.fold_in(key, 11)
    return square_draw(key, DB, SUBW * TOKENS * 0.25, 1.0, 4.0)


def draw_right_stats(key, part):
    key = jax.random.fold_in(key, 12)
    return square_draw(key, SUBW, DB * TOKENS * 0.25, 1.0, 4.0)


def draw_left_roots(key, part):
    key = jax.random.fold_in(key, 13)
    return square_draw(key, DB, (SUBW * TOKENS * 0.25) ** (-0.25), 0.7, 1.4)


def draw_right_roots(key, part):
    key = jax.random.fold_in(key, 14)
    return square_draw(key, SUBW, (DB * TOKENS * 0.25) ** (-0.25), 0.7, 1.4)


def place_ends(values, stream_key, smallest, largest):
    dims = values.shape
    spot = [jax.random.randint(jax.random.fold_in(stream_key, axis), (), 0, dims[axis]) for axis in range(len(dims))]
    values = values.at[tuple(spot)].set(smallest)
    longest = dims.index(max(dims))
    spot[longest] = (spot[longest] + 1) % dims[longest]
    return values.at[tuple(spot)].set(largest)


def block_levels(key, shape, pieces, smallest, top_value):
    level = 1.0
    for axis_at, parts in pieces:
        steps = jax.random.uniform(jax.random.fold_in(jax.random.fold_in(key, 6), axis_at), (parts,), jnp.float32, smallest / len(pieces), top_value / len(pieces))
        level = level * jnp.repeat(jnp.exp(steps), shape[axis_at] // parts).reshape((-1,) + (1,) * (len(shape) - 1 - axis_at))
    return level


def split_up(count, total, most, slope):
    weights = [(1 << 20) // math.isqrt(grade ** slope) + 1 for grade in range(2, count + 1)]
    rest, holding = total - most - (count - 1), [1] * (count - 1)
    while rest > 0:
        free = [i for i in range(count - 1) if holding[i] < most]
        mass, budget = sum([weights[i] for i in free]), rest
        for i in free:
            more = min(most - holding[i], max(1, budget * weights[i] // mass), rest)
            holding[i] = holding[i] + more
            rest = rest - more
    return np.array([most] + holding)


def uneven_parts(stream_key, count, total, bound, lean):
    if count == 2:
        one = jax.random.randint(stream_key, (), max(1, total - bound), min(bound, total - 1) + 1)
        return jnp.stack([one, total - one])
    sizes = jnp.asarray(split_up(count, total, bound, lean), jnp.int32)
    pairs = (count - 1) // 2
    source_of, sink = sizes[1:1 + 2 * pairs:2], sizes[2:2 + 2 * pairs:2]
    margin = jnp.minimum(source_of - 1, bound - sink)
    moved = jax.random.randint(jax.random.fold_in(stream_key, 1), (pairs,), 0, 1 << 20) % (margin + 1)
    sizes = sizes.at[1:1 + 2 * pairs:2].set(source_of - moved).at[2:2 + 2 * pairs:2].set(sink + moved)
    return sizes[jax.random.permutation(jax.random.fold_in(stream_key, 2), count)]


def bell_draw(own_key, extent, deviation, reach, shards=(), kind=jnp.bfloat16):
    values = deviation * jax.random.normal(own_key, extent, jnp.float32)
    if shards:
        values = values * block_levels(own_key, extent, shards, -0.22, 0.18)
    return jnp.clip(values, -reach, reach).astype(kind)


def setup_inputs(seed: int = 0) -> dict:
    key_list = jax.random.split(jax.random.key(seed), 16)
    return {
        "tokens": bell_draw(key_list[0], (TOKENS, MODEL_WIDTH), 1.0, 6.0, ((0, 16),)),
        "cotangent": bell_draw(key_list[1], (TOKENS, MODEL_WIDTH), 1.0, 6.0, ((0, 16),)),
        "segments": jnp.searchsorted(jnp.cumsum(uneven_parts(key_list[2], TOKENS // (2 * TOK_DEV), TOKENS, 8 * TOK_DEV, 2)), jnp.arange(TOKENS), side="right").astype(jnp.int32),
        "padding": place_ends((jax.random.randint(key_list[3], (TOKENS,), 0, 8) < 7).astype(jnp.int32), jax.random.fold_in(key_list[3], 1), 0, 1),
        "owners": jax.vmap(lambda own: jax.random.permutation(own, N_CTX))(jax.random.split(key_list[4], 7)).reshape((7, N_CTX)).astype(jnp.int32),
        "gains": jnp.clip(1.0 + 0.1 * jax.random.normal(key_list[5], (4, MODEL_WIDTH), jnp.float32), 0.5, 1.5),
        "gain_stats": jnp.clip(jnp.exp(jax.random.uniform(key_list[6], (4, MODEL_WIDTH), jnp.float32, math.log(4096.0), math.log(16384.0))), 4096.0, 16384.0),
        "attention_input_master": bell_draw(key_list[7], (MODEL_WIDTH, (QUERY_HEADS + 2 * KEY_VALUE_HEADS) * HEAD_SIZE), MODEL_WIDTH ** -0.5, 0.125, ((0, 4), (1, 8)), jnp.float32),
        "attn_out": bell_draw(key_list[8], (MODEL_WIDTH, QUERY_HEADS * HEAD_SIZE), (QUERY_HEADS * HEAD_SIZE // 16) ** -0.5, 0.5, ((0, 4), (1, 8)), jnp.float32),
        "mlp_in": bell_draw(key_list[9], (MODEL_WIDTH, 2 * FF), MODEL_WIDTH ** -0.5, 0.125, ((0, 4), (1, 8)), jnp.float32),
        "mlp_out": bell_draw(key_list[10], (MODEL_WIDTH, FF), FF ** -0.5, 0.0625, ((0, 4), (1, 8)), jnp.float32),
        "left_stats": draw_left_stats(jax.random.fold_in(key_list[15], 71), 0),
        "right_stats": draw_right_stats(jax.random.fold_in(key_list[15], 71), 0),
        "left_roots": draw_left_roots(jax.random.fold_in(key_list[15], 71), 0),
        "right_roots": draw_right_roots(jax.random.fold_in(key_list[15], 71), 0),
    }


@jax.custom_vjp
def low(v):
    return lax.optimization_barrier(v.astype(jnp.bfloat16)).astype(jnp.float32)

@jax.custom_vjp
def reduced_backward(v):
    return v

def low_keep(v):
    return (low(v), None)

def low_pass(kept, grad):
    return (grad,)

def back_keep(v):
    return (v, None)

def back_low(kept, grad):
    return (low(grad),)
low.defvjp(low_keep, low_pass)
reduced_backward.defvjp(back_keep, back_low)
norm_eps = 1e-06
soft_cap = 50.0
stat_decay = 0.5
master_rate = 0.25
gain_rate = 0.3
rope_base = 10000.0
highest = lax.Precision.HIGHEST

def matrix_multiply(left, right):
    return jnp.dot(left, right, precision=highest, preferred_element_type=jnp.float32)

def rms_norm(values, gain):
    return values * lax.rsqrt(lax.optimization_barrier(jnp.mean(values * values, axis=-1, keepdims=True)) + norm_eps) * gain

def rotation(positions):
    half = HEAD_SIZE // 2
    freqs = jnp.exp(jnp.arange(half, dtype=jnp.float32) * (-2.0 * math.log(rope_base) / HEAD_SIZE))
    angles = positions.astype(jnp.float32)[:, None] * freqs[None, :]
    return (jnp.cos(angles), jnp.sin(angles))

def rotate(values, cosine, sine):
    half = values.shape[-1] // 2
    first = values[..., :half]
    second = values[..., half:]
    cosine = cosine[:, None, :]
    sine = sine[:, None, :]
    return jnp.concatenate([first * cosine - second * sine, second * cosine + first * sine], axis=-1)

def unpack(packed, widths, orders):
    grouped = packed.reshape(MODEL_WIDTH, N_CTX, N_MP, packed.shape[1] // (N_CTX * N_MP))
    result = []
    offset = 0
    for width_part, order in zip(widths, orders):
        part = grouped[:, :, :, offset:offset + width_part]
        part = jnp.take(part, jnp.argsort(order).astype(jnp.int32), axis=1)
        result.append(jnp.transpose(part, (0, 2, 1, 3)).reshape(MODEL_WIDTH, N_MP * N_CTX * width_part))
        offset = offset + width_part
    return result

def attend(queries, keys, values, segment, present):
    block_rows = min(512, PACKED_TOKENS)
    blocks = PACKED_TOKENS // block_rows
    keys_ext = jnp.concatenate([jnp.zeros((WINDOW, QUERY_HEADS, HEAD_SIZE), jnp.float32), keys], axis=0)
    values_ext = jnp.concatenate([jnp.zeros((WINDOW, QUERY_HEADS, HEAD_SIZE), jnp.float32), values], axis=0)
    segment = segment.astype(jnp.int32)
    segment_ext = jnp.concatenate([jnp.full((WINDOW,), -1, jnp.int32), segment])
    present_ext = jnp.concatenate([jnp.zeros((WINDOW,), jnp.int32), present.astype(jnp.int32)])
    scale = HEAD_SIZE ** (-0.5)

    def block(number):
        first = number * block_rows
        query_part = lax.dynamic_slice_in_dim(queries, first, block_rows, 0)
        key_part = lax.dynamic_slice_in_dim(keys_ext, first, block_rows + WINDOW, 0)
        value_part = lax.dynamic_slice_in_dim(values_ext, first, block_rows + WINDOW, 0)
        query_pos = first + jnp.arange(block_rows, dtype=jnp.int32)
        key_pos = first - WINDOW + jnp.arange(block_rows + WINDOW, dtype=jnp.int32)
        query_seg = lax.dynamic_slice_in_dim(segment, first, block_rows, 0)
        key_seg = lax.dynamic_slice_in_dim(segment_ext, first, block_rows + WINDOW, 0)
        key_present = lax.dynamic_slice_in_dim(present_ext, first, block_rows + WINDOW, 0)
        visible = (key_pos[None, :] >= 0) & (key_pos[None, :] <= query_pos[:, None])
        visible = visible & (query_pos[:, None] - key_pos[None, :] < WINDOW)
        visible = visible & (query_seg[:, None] == key_seg[None, :])
        visible = visible & ((key_present[None, :] == 1) | (key_pos[None, :] == query_pos[:, None]))
        raw = reduced_backward(jnp.einsum('qhd,khd->hqk', query_part, key_part, precision=highest) * scale)
        capped = jnp.where(visible[None], soft_cap * jnp.tanh(raw / soft_cap), -1e+30)
        top = lax.optimization_barrier(jnp.max(capped, axis=-1, keepdims=True))
        expo = jnp.exp(capped - top)
        probs = low(expo / lax.optimization_barrier(jnp.sum(expo, axis=-1, keepdims=True)))
        return jnp.einsum('hqk,khd->qhd', probs, value_part, precision=highest)
    result = lax.map(jax.checkpoint(block), jnp.arange(blocks, dtype=jnp.int32))
    return result.reshape(PACKED_TOKENS, QUERY_HEADS, HEAD_SIZE)

def layer(inputs, gain_rows, attention_input_master, attn_out, mlp_in, mlp_out, owners, segments, padding):
    key_columns = KEY_VALUE_HEADS * HEAD_SIZE // (N_CTX * N_MP)
    ffn_cols = FF // (N_CTX * N_MP)
    w_query, key_weight, value_weight = unpack(low(attention_input_master), (HEAD_SIZE, key_columns, key_columns), (owners[0], owners[1], owners[2]))
    w_output = unpack(low(attn_out), (HEAD_SIZE,), (owners[3],))[0]
    w_gate, w_up = unpack(low(mlp_in), (ffn_cols, ffn_cols), (owners[4], owners[5]))
    w_down = unpack(low(mlp_out), (ffn_cols,), (owners[6],))[0]
    cosine, sine = rotation(jnp.arange(PACKED_TOKENS, dtype=jnp.int32))
    head_group = QUERY_HEADS // KEY_VALUE_HEADS

    def sequence(packed_args):
        current, segment, present = packed_args
        hidden_state = low(rms_norm(current, gain_rows[0]))
        query_pre = reduced_backward(matrix_multiply(hidden_state, w_query)).reshape(PACKED_TOKENS, QUERY_HEADS, HEAD_SIZE)
        key_before_rotation = reduced_backward(matrix_multiply(hidden_state, key_weight)).reshape(PACKED_TOKENS, KEY_VALUE_HEADS, HEAD_SIZE)
        value_projected = reduced_backward(matrix_multiply(hidden_state, value_weight)).reshape(PACKED_TOKENS, KEY_VALUE_HEADS, HEAD_SIZE)
        queries = reduced_backward(low(rotate(query_pre, cosine, sine)))
        keys = reduced_backward(jnp.repeat(low(rotate(key_before_rotation, cosine, sine)), head_group, axis=1))
        values = reduced_backward(jnp.repeat(low(value_projected), head_group, axis=1))
        attended = reduced_backward(low(attend(queries, keys, values, segment, present))).reshape(PACKED_TOKENS, QUERY_HEADS * HEAD_SIZE)
        attn = reduced_backward(jnp.einsum('tq,dq->td', attended, w_output, precision=highest))
        mixed = current + rms_norm(attn, gain_rows[1])
        hidden_two = low(rms_norm(mixed, gain_rows[2]))
        gate = reduced_backward(matrix_multiply(hidden_two, w_gate))
        upper = reduced_backward(matrix_multiply(hidden_two, w_up))
        active = low(jax.nn.gelu(gate, approximate=True) * upper)
        moved = reduced_backward(jnp.einsum('tf,df->td', active, w_down, precision=highest))
        return mixed + rms_norm(moved, gain_rows[3])
    count = TOKENS // PACKED_TOKENS
    result = lax.map(sequence, (inputs.reshape(count, PACKED_TOKENS, MODEL_WIDTH), segments.reshape(count, PACKED_TOKENS), padding.reshape(count, PACKED_TOKENS)))
    return result.reshape(TOKENS, MODEL_WIDTH)

def to_blocks(grad):
    cols = grad.shape[1] // (N_CTX * N_MP)
    split = grad.reshape(N_DP, MODEL_WIDTH // N_DP, N_CTX, N_MP, cols // SUBW, SUBW)
    return jnp.transpose(split, (0, 2, 3, 4, 1, 5))

def from_blocks(blocks, cols):
    return jnp.transpose(blocks, (0, 4, 1, 2, 3, 5)).reshape(MODEL_WIDTH, N_CTX * N_MP * cols)

def reference(tokens, cotangent, segments, padding, owners, gains, gain_stats, attention_input_master, attn_out, mlp_in, mlp_out, left_stats, right_stats, left_roots, right_roots):

    def forward(inputs, gain_rows, first_in, first_out, second_in, second_out):
        return layer(inputs, gain_rows, first_in, first_out, second_in, second_out, owners, segments, padding)
    outputs, pullback = jax.vjp(forward, tokens.astype(jnp.float32), gains, attention_input_master, attn_out, mlp_in, mlp_out)
    grads = pullback(cotangent.astype(jnp.float32))
    input_grad = grads[0]
    gain_grad = grads[1]
    weight_grads = grads[2:]
    masters = (attention_input_master, attn_out, mlp_in, mlp_out)
    blocks = [to_blocks(grad) for grad in weight_grads]
    counts = [part.shape[3] for part in blocks]
    stacked = jnp.concatenate(blocks, axis=3)
    new_left = stat_decay * left_stats + (1.0 - stat_decay) * jnp.einsum('...rs,...qs->...rq', stacked, stacked, precision=highest)
    new_right = stat_decay * right_stats + (1.0 - stat_decay) * jnp.einsum('...rs,...rq->...sq', stacked, stacked, precision=highest)
    step = jnp.einsum('...rq,...qs->...rs', left_roots, stacked, precision=highest)
    step = jnp.einsum('...rs,...sq->...rq', step, right_roots, precision=highest)
    updated = []
    offset = 0
    for master, count in zip(masters, counts):
        part = step[:, :, :, offset:offset + count]
        updated.append(master - master_rate * from_blocks(part, master.shape[1] // (N_CTX * N_MP)))
        offset = offset + count
    new_gain_stats = stat_decay * gain_stats + (1.0 - stat_decay) * gain_grad * gain_grad
    new_gains = gains - gain_rate * gain_grad * lax.rsqrt(new_gain_stats)
    return (outputs.astype(jnp.bfloat16), input_grad, weight_grads[0], weight_grads[1], weight_grads[2], weight_grads[3], updated[0], updated[1], updated[2], updated[3], new_left, new_right, gain_grad, new_gain_stats, new_gains)
```

```python
import math

import jax
import jax.numpy as jnp
from jax import lax
from jax.sharding import PartitionSpec as P

HEAD_SIZE = 256
QUERY_HEADS = 8
KEY_VALUE_HEADS = 4
PACKED_TOKENS = 4096
WINDOW = 1024
SUBW = 128


norm_eps = 1e-06
soft_cap = 50.0
stat_decay = 0.5
master_rate = 0.25
gain_rate = 0.3
rope_base = 10000.0
highest = lax.Precision.HIGHEST


def shifted(block, axis, distance):
    devices = range(lax.axis_size(axis))
    route = [(i - distance, i) for i in devices if i - distance in devices]
    return lax.ppermute(block, axis, route)


def normalize(values, gain):
    scale = lax.rsqrt(jnp.mean(values * values, axis=-1, keepdims=True) + norm_eps)
    normed = values * scale
    return (normed * gain, normed, scale)


def norm_back(normed, scale, gain, upstream):
    gain_part = jnp.sum(upstream * normed, axis=0)
    inner = upstream * gain
    return (scale * (inner - normed * jnp.mean(inner * normed, axis=-1, keepdims=True)), gain_part)


def rotation(positions):
    half = HEAD_SIZE // 2
    freqs = jnp.exp(jnp.arange(half, dtype=jnp.float32) * (-2.0 * math.log(rope_base) / HEAD_SIZE))
    angles = positions.astype(jnp.float32)[:, None] * freqs[None, :]
    return (jnp.cos(angles), jnp.sin(angles))


def rotate(values, cosine, sine):
    half = values.shape[-1] // 2
    first = values[..., :half]
    second = values[..., half:]
    cosine = cosine[:, None, :]
    sine = sine[:, None, :]
    return jnp.concatenate(
        [first * cosine - second * sine, second * cosine + first * sine], axis=-1
    )


def rotate_back(grads, cosine, sine):
    half = grads.shape[-1] // 2
    first = grads[..., :half]
    second = grads[..., half:]
    cosine = cosine[:, None, :]
    sine = sine[:, None, :]
    return jnp.concatenate(
        [first * cosine + second * sine, second * cosine - first * sine], axis=-1
    )


def inverse(order, count):
    slots = jnp.arange(count, dtype=jnp.int32)
    matches = order[None, :] == slots[:, None]
    return jnp.sum(jnp.where(matches, slots[None, :], 0), axis=1)


def dot(left, right):
    return lax.dot_general(
        left, right, (((1,), (0,)), ((), ())), preferred_element_type=jnp.float32
    )


def dot_nt(left, right):
    return lax.dot_general(
        left, right, (((1,), (1,)), ((), ())), preferred_element_type=jnp.float32
    )


def dot_tn(left, right):
    return lax.dot_general(
        left, right, (((0,), (0,)), ((), ())), preferred_element_type=jnp.float32
    )


def swap(block):
    return lax.ppermute(block, "mp", [(0, 1), (1, 0)])


def cycle(block, axis, distance):
    count = lax.axis_size(axis)
    return lax.ppermute(block, axis, [(i, (i + distance) % count) for i in range(count)])


def tie(value, *others):
    return lax.optimization_barrier((value,) + others)[0]


def pick(blocks, index):
    return lax.dynamic_index_in_dim(blocks, index, 0, keepdims=False, allow_negative_indices=False)


def wrap(index, count):
    return index & (count - 1) if count & (count - 1) == 0 else lax.rem(index, count)


def gather_ctx(block):
    blocks = [block]
    for _ in range(lax.axis_size("ctx") - 1):
        blocks.append(cycle(blocks[-1], "ctx", 1))
    return blocks


def scatter_ctx(parts, steps=None):
    total = parts[1]
    for part in parts[2:] + parts[:1]:
        sent = total.astype(jnp.bfloat16)
        if steps is not None:
            steps.append(sent)
        arrived = cycle(sent, "ctx", 1)
        total = arrived.astype(jnp.float32) + part
    return total


def gather_ctx_direct(block):
    return [block] + [cycle(block, "ctx", s) for s in range(1, lax.axis_size("ctx"))]


def scatter_ctx_direct(parts):
    total = parts[0]
    for s in range(1, len(parts)):
        arrived = cycle(parts[s].astype(jnp.bfloat16), "ctx", -s)
        total = total + arrived.astype(jnp.float32)
    return total


def neighbour(block, bit):
    return lax.ppermute(block, "dp", [(i, i ^ bit) for i in range(4)])


def gather_dp(block):
    count = lax.axis_size("dp")
    rows, cols = block.shape
    if count != 4:
        return lax.all_gather(block, "dp", axis=0, tiled=True)
    half = rows // 2
    index = lax.axis_index("dp")
    along_x = neighbour(block, 1)
    along_y = neighbour(block, 2)
    far_first = neighbour(along_x[:half], 2)
    far_second = neighbour(along_y[half:], 1)
    whole = jnp.zeros((count, rows, cols), block.dtype)

    def place(whole, part, where, start):
        return lax.dynamic_update_slice(
            whole, part[None], (where, 0 * where + start, 0 * where), allow_negative_indices=False
        )

    whole = place(whole, block, index, 0)
    whole = place(whole, along_x, index ^ 1, 0)
    whole = place(whole, along_y, index ^ 2, 0)
    whole = place(whole, far_first, index ^ 3, 0)
    whole = place(whole, far_second, index ^ 3, half)
    return whole.reshape(count * rows, cols)


def scatter_dp(terms, *others):
    count = lax.axis_size("dp")
    rows, cols = terms.shape[0] // count, terms.shape[1]
    if count != 4:
        return lax.psum_scatter(terms, "dp", scatter_dimension=0, tiled=True).astype(jnp.float32)
    half = rows // 2
    index = lax.axis_index("dp")
    terms = terms.reshape(count, rows, cols)
    wide = lambda value: value.astype(jnp.float32)
    far = pick(terms, index ^ 3)
    from_x = neighbour(far[:half], 1)
    from_y = neighbour(far[half:], 2)
    to_x = wide(pick(terms, index ^ 1))
    to_y = wide(pick(terms, index ^ 2))
    if others:
        from_y = tie(from_y, *others)
        from_x = tie(from_x, *others)
    to_x = jnp.concatenate([to_x[:half], to_x[half:] + wide(from_y)]).astype(jnp.bfloat16)
    to_y = jnp.concatenate([to_y[:half] + wide(from_x), to_y[half:]]).astype(jnp.bfloat16)
    return wide(pick(terms, index)) + wide(neighbour(to_x, 1)) + wide(neighbour(to_y, 2))


def sum_all(block):
    block = block + swap(block)
    for axis in ("ctx", "dp"):
        count = lax.axis_size(axis)
        terms = jnp.stack([block] + [cycle(block, axis, s) for s in range(1, count)])
        index = lax.axis_index(axis)
        block = sum(pick(terms, wrap(index + count - j, count)) for j in range(count))
    return block


GROUPS = 3


def combine(weights, blocks):
    return sum(weights[k] * blocks[k].astype(jnp.float32) for k in range(len(blocks)))


def fold(block):
    tall = block.shape[0] // GROUPS
    return jnp.concatenate([block[g * tall : (g + 1) * tall] for g in range(GROUPS)], axis=1)


def unfold(block):
    wide = block.shape[1] // GROUPS
    return jnp.concatenate([block[:, g * wide : (g + 1) * wide] for g in range(GROUPS)], axis=0)


ATTEND_ROWS = 512


def seen_part(queries, keys, query_code, key_code, number):
    start = number * ATTEND_ROWS
    span = slice(start, start + ATTEND_ROWS + WINDOW)
    here = slice(start, start + ATTEND_ROWS)
    raw = dot_nt(queries[here], keys[span]) * HEAD_SIZE ** (-0.5)
    bent = jnp.tanh(raw * (1.0 / soft_cap))
    row = lax.broadcasted_iota(jnp.int32, raw.shape, 0)
    col = lax.broadcasted_iota(jnp.int32, raw.shape, 1)
    visible = (query_code[here] == key_code[:, span]) & (col > row) & (col <= row + WINDOW)
    visible = visible | (col == row + WINDOW)
    return here, span, jnp.where(visible, jnp.exp(soft_cap * bent), 0.0), bent


def attend_forward(queries, both, prev_both, query_code, key_code):
    joined = jnp.concatenate([prev_both, both], axis=0)
    keys, values = joined[:, :HEAD_SIZE], joined[:, HEAD_SIZE:]
    outs, sums = [], []
    for number in range(queries.shape[0] // ATTEND_ROWS):
        _, span, expo, _ = seen_part(queries, keys, query_code, key_code, number)
        total = jnp.sum(expo, axis=1, keepdims=True)
        outs.append(dot(expo.astype(jnp.bfloat16), values[span]) / total)
        sums.append(total)
    out = jnp.concatenate(outs, axis=0)
    return out.astype(jnp.bfloat16), out, jnp.concatenate(sums, axis=0)


def attend_backward(queries, both, prev_both, query_code, key_code, grads, full, sums):
    rows = queries.shape[0]
    scale = HEAD_SIZE ** (-0.5)
    joined = jnp.concatenate([prev_both, both], axis=0)
    keys, values = joined[:, :HEAD_SIZE], joined[:, HEAD_SIZE:]
    query_grads, pieces = [], []
    for number in range(rows // ATTEND_ROWS):
        here, span, expo, bent = seen_part(queries, keys, query_code, key_code, number)
        probs = expo * (1.0 / sums[here])
        prob_grad = dot_nt(grads[here], values[span])
        delta = jnp.sum(grads[here].astype(jnp.float32) * full[here], axis=1, keepdims=True)
        score = (probs * (prob_grad - delta) * (1.0 - bent * bent)).astype(jnp.bfloat16)
        query_grads.append(dot(score, keys[span]) * scale)
        part = jnp.concatenate(
            [dot_tn(score, queries[here]) * scale, dot_tn(probs.astype(jnp.bfloat16), grads[here])],
            axis=1,
        )
        pieces.append(jnp.pad(part, ((span.start, 2 * rows - span.stop), (0, 0))))
    total = sum(pieces)
    return (
        jnp.concatenate(query_grads, axis=0),
        total[rows:],
        total[:rows].astype(jnp.bfloat16),
    )


def body(
    tokens,
    cotangent,
    segments,
    padding,
    owners,
    gains,
    gain_stats,
    attention_input_master,
    attn_out,
    mlp_in,
    mlp_out,
    left_stats,
    right_stats,
    left_roots,
    right_roots,
):
    nctx = lax.axis_size("ctx")
    ctx_index = lax.axis_index("ctx")
    dp_index = lax.axis_index("dp")
    mp_index = lax.axis_index("mp")
    rows, width = tokens.shape
    half = rows // 2
    group_rows = rows * nctx
    dblock = attention_input_master.shape[0]
    key_columns = (attention_input_master.shape[1] - HEAD_SIZE) // 2
    ffn_cols = mlp_out.shape[1]
    piece = ffn_cols // nctx
    per_head = HEAD_SIZE // key_columns
    head_group = QUERY_HEADS // KEY_VALUE_HEADS
    before = lambda s: wrap(ctx_index + nctx - s, nctx)
    slots = jnp.arange(nctx, dtype=jnp.int32)
    one = lambda condition: condition.astype(jnp.float32)
    held = one(owners[:, None, :] == slots[None, :, None])
    turned_to = one(slots[None, :] == ((ctx_index + nctx - slots) % nctx)[:, None])
    my_query = jnp.sum(held[0] * turned_to[0][None, :], axis=1)
    key_weights, value_weights = [], []
    for part in range(per_head):
        wanted = one(slots[:, None] == (slots // head_group * per_head + part)[None, :])
        column = jnp.sum(wanted * my_query[None, :], axis=1)
        for row, weights in ((1, key_weights), (2, value_weights)):
            holder = jnp.sum(held[row] * column[:, None], axis=0)
            weights.append(jnp.sum(turned_to * holder[None, :], axis=1))
    paired = jnp.sum(held[0][:, :, None] * held[3][:, None, :], axis=0)
    paired_back = jnp.sum(paired[:, None, :] * turned_to[None, :, :], axis=2)

    def halves(block):
        pair = block.reshape((2, block.shape[0] // 2) + block.shape[1:])
        return jnp.where(mp_index == 0, pair, pair[::-1]).reshape(block.shape)

    def own_half(block):
        return lax.dynamic_slice_in_dim(block, mp_index * half, half, 0, allow_negative_indices=False)

    def other_half(block):
        return lax.dynamic_slice_in_dim(
            block, (1 - mp_index) * half, half, 0, allow_negative_indices=False
        )

    def both(block):
        return jnp.concatenate([block, swap(block)], axis=0)

    def in_order(blocks):
        stacked = jnp.stack(blocks)
        return jnp.concatenate([pick(stacked, before(j)) for j in range(nctx)], axis=0)

    def reduce_width(parts, steps=None):
        terms = []
        for part in parts:
            arrived = swap(part[half:].astype(jnp.bfloat16)).astype(jnp.float32)
            terms.append(part[:half] + arrived)
        return scatter_ctx(terms, steps)

    key_value = gather_ctx_direct(attention_input_master[:, HEAD_SIZE:].astype(jnp.bfloat16))
    low_in = [attention_input_master[:, :HEAD_SIZE]]
    for start, table in ((0, key_weights), (key_columns, value_weights)):
        parts = [block[:, start : start + key_columns] for block in key_value]
        low_in += [combine(weights, parts) for weights in table]
    whole_in = gather_dp(jnp.concatenate(low_in, axis=1).astype(jnp.bfloat16))

    def pass_on(block):
        return lax.all_to_all(block, "ctx", split_axis=0, concat_axis=0, tiled=True)

    def quarters_of(block):
        return [block[:, k * piece : (k + 1) * piece] for k in range(nctx)]

    def spread(master, column, row, *others):
        block = master if column is None else master[:, column[0] : column[0] + column[1]]
        dealt = jnp.stack([fold(quarter) for quarter in quarters_of(block.astype(jnp.bfloat16))])
        came = pass_on(tie(dealt, *others))
        blocks = [
            unfold(combine(held[row][b], [came[k] for k in range(nctx)]).astype(jnp.bfloat16))
            for b in range(nctx)
        ]
        return came, jnp.concatenate(blocks, axis=1)

    gate_came, low_gate = spread(mlp_in, (0, ffn_cols), 4, *key_value[1:])
    whole_gate = gather_dp(low_gate)
    out_blocks = gather_ctx_direct(tie(attn_out.astype(jnp.bfloat16), gate_came))
    whole_out = gather_dp(
        jnp.concatenate([combine(paired_back[j], out_blocks) for j in range(nctx)], axis=1).astype(
            jnp.bfloat16
        )
    )

    inputs = own_half(tokens).astype(jnp.float32)
    first_out, first_normed, first_scale = normalize(inputs, gains[0])
    first_blocks = gather_ctx(tie(first_out.astype(jnp.bfloat16), out_blocks[2]))
    hidden_in = [both(block) for block in first_blocks]
    _, low_up = spread(mlp_in, (ffn_cols, ffn_cols), 5, first_blocks[3])
    whole_up = gather_dp(low_up)
    _, low_down = spread(mlp_out, None, 6, first_blocks[3])
    whole_down = gather_dp(low_down)
    projected = in_order([halves(dot(block, whole_in)) for block in hidden_in])
    group_first = dp_index * group_rows
    group_pos = group_first + jnp.arange(group_rows, dtype=jnp.int32)
    cosine, sine = rotation(group_pos % PACKED_TOKENS)
    turned = rotate(
        projected[:, : 2 * HEAD_SIZE].reshape(group_rows, 2, HEAD_SIZE), cosine, sine
    ).astype(jnp.bfloat16)
    queries_h = turned[:, 0]
    both_h = jnp.concatenate(
        [turned[:, 1], projected[:, 2 * HEAD_SIZE :].astype(jnp.bfloat16)], axis=1
    )
    prev_both = shifted(both_h, "dp", 1)
    codes = segments + PACKED_TOKENS * (
        jnp.arange(segments.shape[0], dtype=jnp.int32) // PACKED_TOKENS
    )
    nobody = jnp.full((group_rows,), -1, jnp.int32)
    key_codes = jnp.concatenate([nobody, jnp.where(padding == 1, codes, -1)])
    key_code = lax.dynamic_slice_in_dim(
        key_codes, group_first, 2 * group_rows, 0, allow_negative_indices=False
    )[None, :]
    query_code = lax.dynamic_slice_in_dim(
        codes, group_first, group_rows, 0, allow_negative_indices=False
    )[:, None]
    attended_low, attended, prob_sums = attend_forward(
        tie(queries_h, low_up), both_h, prev_both, query_code, key_code
    )
    came = pass_on(attended_low.reshape(nctx, rows, HEAD_SIZE))
    heads_out = jnp.concatenate([came[j] for j in range(nctx)], axis=1)
    attn_part = dot_nt(tie(heads_out, low_down), whole_out)
    attn = own_half(attn_part) + swap(other_half(attn_part).astype(jnp.bfloat16)).astype(
        jnp.float32
    )
    second_out, second_normed, second_scale = normalize(attn, gains[1])
    mixed = inputs + second_out
    third_out, third_normed, third_scale = normalize(mixed, gains[2])

    hidden_two = [both(block) for block in gather_ctx(third_out.astype(jnp.bfloat16))]
    pulls, actives, uppers, gelus, moved_parts = [], [], [], [], []
    for block in hidden_two:
        gate = dot(block, whole_gate)
        upper = dot(block, whole_up)
        gelu_value, gelu_pull = jax.vjp(lambda values: jax.nn.gelu(values, approximate=True), gate)
        active = (gelu_value * upper).astype(jnp.bfloat16)
        pulls.append(gelu_pull)
        actives.append(active)
        uppers.append(upper)
        gelus.append(gelu_value)
        moved_parts.append(dot_nt(active, whole_down))
    moved = reduce_width(moved_parts)
    fourth_out, fourth_normed, fourth_scale = normalize(moved, gains[3])
    block_out = halves(both((mixed + fourth_out).astype(jnp.bfloat16)))
    upstream = own_half(cotangent).astype(jnp.float32)
    moved_grad, fourth_gain = norm_back(fourth_normed, fourth_scale, gains[3], upstream)
    moved_low = [both(block) for block in gather_ctx(moved_grad.astype(jnp.bfloat16))]
    gate_grads, upper_grads, hidden_two_parts = [], [], []
    for s, block in enumerate(moved_low):
        active_grad = dot(block, whole_down)
        gate_grad = pulls[s](active_grad * uppers[s])[0].astype(jnp.bfloat16)
        upper_grad = (active_grad * gelus[s]).astype(jnp.bfloat16)
        gate_grads.append(gate_grad)
        upper_grads.append(upper_grad)
        hidden_two_parts.append(dot_nt(gate_grad, whole_gate) + dot_nt(upper_grad, whole_up))
    steps = []
    hidden_two_grad = reduce_width(hidden_two_parts, steps)
    cat = lambda values: jnp.concatenate(values, axis=0)
    low = lambda values: values.astype(jnp.bfloat16)
    down_terms = low(dot_tn(cat(moved_low), cat(actives)))
    hidden_two_all = cat(hidden_two)
    gate_terms = low(dot_tn(hidden_two_all, tie(cat(gate_grads), steps[1])))
    up_terms = low(dot_tn(hidden_two_all, tie(cat(upper_grads), steps[2])))
    down_sum = scatter_dp(down_terms)
    gate_sum = scatter_dp(gate_terms)

    def collect(summed, row):
        quarters = quarters_of(summed)
        dealt = [fold(low(combine(held[row][:, k], quarters))) for k in range(nctx)]
        came = pass_on(jnp.stack(dealt))
        return came, jnp.concatenate([unfold(came[j]) for j in range(nctx)], axis=1).astype(
            jnp.float32
        )

    mixed_part, third_gain = norm_back(third_normed, third_scale, gains[2], hidden_two_grad)
    mixed_grad = upstream + mixed_part
    attn_grad, second_gain = norm_back(second_normed, second_scale, gains[1], mixed_grad)
    attn_low = halves(both(attn_grad.astype(jnp.bfloat16)))
    heads_grad = low(dot(attn_low, whole_out))

    head_grad = pass_on(
        jnp.stack([heads_grad[:, j * HEAD_SIZE : (j + 1) * HEAD_SIZE] for j in range(nctx)])
    ).reshape(group_rows, HEAD_SIZE)

    query_grads, both_own, both_prev = attend_backward(
        queries_h, both_h, prev_both, query_code, key_code, head_grad, attended, prob_sums
    )
    both_next = shifted(both_prev, "dp", -1)
    up_sum = scatter_dp(up_terms, both_next)
    down_came, down_grad = collect(tie(down_sum, head_grad), 6)
    gate_came, gate_grad_whole = collect(tie(gate_sum, down_came), 4)
    up_came, up_grad_whole = collect(tie(up_sum, gate_came), 5)
    both_total = both_own + both_next.astype(jnp.float32)
    turned_back = rotate_back(
        jnp.stack([query_grads, both_total[:, :HEAD_SIZE]], axis=1), cosine, sine
    ).reshape(group_rows, 2 * HEAD_SIZE)
    right_attn = low(jnp.concatenate([turned_back, both_total[:, HEAD_SIZE:]], axis=1)).reshape(
        nctx, rows, 3 * HEAD_SIZE
    )
    right_attn = cat([halves(pick(right_attn, before(s))) for s in range(nctx)])
    parts = [dot_nt(right_attn[s * rows : (s + 1) * rows], whole_in) for s in range(nctx)]
    terms = [part[:half] + swap(low(part[half:])).astype(jnp.float32) for part in parts]
    sent_one = low(terms[1])
    sent_two = low(cycle(sent_one, "ctx", 1).astype(jnp.float32) + terms[2])
    sent_two = tie(sent_two, gate_came)
    sent_three = low(cycle(sent_two, "ctx", 1).astype(jnp.float32) + terms[3])
    hidden_grad = cycle(sent_three, "ctx", 1).astype(jnp.float32) + terms[0]
    input_part, first_gain = norm_back(first_normed, first_scale, gains[0], hidden_grad)
    input_grad = halves(both(mixed_grad + input_part))

    out_sum = scatter_dp(low(dot_tn(tie(attn_low, sent_one), heads_out)))
    in_terms = low(dot_tn(cat(hidden_in), tie(right_attn, sent_one)))
    in_sum = scatter_dp(in_terms)
    heads = [out_sum[:, j * HEAD_SIZE : (j + 1) * HEAD_SIZE] for j in range(nctx)]
    heads[0] = tie(heads[0], up_came)
    out_grad = scatter_ctx_direct([combine(paired_back[:, s], heads) for s in range(nctx)])
    sums = [
        in_sum[:, start + p * key_columns : start + (p + 1) * key_columns]
        for start in (HEAD_SIZE, 2 * HEAD_SIZE)
        for p in range(per_head)
    ]
    key_value_grad = scatter_ctx_direct(
        [
            jnp.concatenate(
                [
                    sum(weights[s] * block for weights, block in zip(table, blocks))
                    for table, blocks in (
                        (key_weights, sums[:per_head]),
                        (value_weights, sums[per_head:]),
                    )
                ],
                axis=1,
            )
            for s in range(nctx)
        ]
    )
    grad_attn_in = jnp.concatenate([in_sum[:, :HEAD_SIZE], key_value_grad], axis=1)
    grad_mlp_in = jnp.concatenate([gate_grad_whole, up_grad_whole], axis=1)

    gain_grad = sum_all(jnp.stack([first_gain, second_gain, third_gain, fourth_gain], axis=0))
    new_gain_stats = stat_decay * gain_stats + (1.0 - stat_decay) * gain_grad * gain_grad
    new_gains = gains - gain_rate * gain_grad * lax.rsqrt(new_gain_stats)

    stats = tuple(
        value.reshape(value.shape[3:])
        for value in (left_stats, right_stats, left_roots, right_roots)
    )
    in_blocks = attention_input_master.shape[1] // SUBW
    out_count = attn_out.shape[1] // SUBW
    ffn_blocks = ffn_cols // SUBW
    first = in_blocks + out_count
    masters = (attention_input_master, attn_out, mlp_in, mlp_out)
    grads = (grad_attn_in, out_grad, grad_mlp_in, down_grad)
    pieces = [
        jnp.transpose(grad.reshape(dblock, grad.shape[1] // SUBW, SUBW), (1, 0, 2))
        for grad in grads
    ]
    stacked = low(jnp.concatenate(pieces, axis=0))
    batched = lambda left, right, sum_left, sum_right: lax.dot_general(
        left, right, (((sum_left,), (sum_right,)), ((0,), (0,))), preferred_element_type=jnp.float32
    )
    new_left = stat_decay * stats[0] + (1.0 - stat_decay) * batched(stacked, stacked, 2, 2)
    new_right = stat_decay * stats[1] + (1.0 - stat_decay) * batched(stacked, stacked, 1, 1)
    step = batched(low(batched(low(stats[2]), stacked, 2, 1)), low(stats[3]), 2, 1)
    updated = []
    offset = 0
    for master in masters:
        count = master.shape[1] // SUBW
        part = jnp.transpose(step[offset : offset + count], (1, 0, 2))
        updated.append(master - master_rate * part.reshape(dblock, master.shape[1]))
        offset = offset + count
    new_attn_in, new_attn_out, new_mlp_in, new_mlp_out = updated
    return (
        block_out,
        input_grad,
        grad_attn_in,
        out_grad,
        grad_mlp_in,
        down_grad,
        new_attn_in,
        new_attn_out,
        new_mlp_in,
        new_mlp_out,
        new_left.reshape(left_stats.shape),
        new_right.reshape(right_stats.shape),
        gain_grad,
        new_gain_stats,
        new_gains,
    )


def solution(mesh):
    return jax.shard_map(
        body,
        mesh=mesh,
        in_specs=(
            P(("dp", "ctx"), None),
            P(("dp", "ctx"), None),
            P(),
            P(),
            P(),
            P(),
            P(),
            P("dp", ("ctx", "mp")),
            P("dp", ("ctx", "mp")),
            P("dp", ("ctx", "mp")),
            P("dp", ("ctx", "mp")),
            P("dp", "ctx", "mp", None, None, None),
            P("dp", "ctx", "mp", None, None, None),
            P("dp", "ctx", "mp", None, None, None),
            P("dp", "ctx", "mp", None, None, None),
        ),
        out_specs=(
            P(("dp", "ctx"), None),
            P(("dp", "ctx"), None),
            P("dp", ("ctx", "mp")),
            P("dp", ("ctx", "mp")),
            P("dp", ("ctx", "mp")),
            P("dp", ("ctx", "mp")),
            P("dp", ("ctx", "mp")),
            P("dp", ("ctx", "mp")),
            P("dp", ("ctx", "mp")),
            P("dp", ("ctx", "mp")),
            P("dp", "ctx", "mp", None, None, None),
            P("dp", "ctx", "mp", None, None, None),
            P(),
            P(),
            P(),
        ),
        check_vma=False,
    )
```

```python
import math

import jax
import jax.numpy as jnp
from jax import lax
from jax.sharding import PartitionSpec as P

HEAD_SIZE = 256
QUERY_HEADS = 8
KEY_VALUE_HEADS = 4
PACKED_TOKENS = 4096
WINDOW = 1024
SUBW = 128


norm_eps = 1e-06
soft_cap = 50.0
stat_decay = 0.5
master_rate = 0.25
gain_rate = 0.3
rope_base = 10000.0
highest = lax.Precision.HIGHEST


def shifted(block, axis, distance):
    devices = range(lax.axis_size(axis))
    route = [(i - distance, i) for i in devices if i - distance in devices]
    return lax.ppermute(block, axis, route)


def normalize(values, gain):
    scale = lax.rsqrt(jnp.mean(values * values, axis=-1, keepdims=True) + norm_eps)
    normed = values * scale
    return (normed * gain, normed, scale)


def norm_back(normed, scale, gain, upstream):
    gain_part = jnp.sum(upstream * normed, axis=0)
    inner = upstream * gain
    return (scale * (inner - normed * jnp.mean(inner * normed, axis=-1, keepdims=True)), gain_part)


def rotation(positions):
    half = HEAD_SIZE // 2
    freqs = jnp.exp(jnp.arange(half, dtype=jnp.float32) * (-2.0 * math.log(rope_base) / HEAD_SIZE))
    angles = positions.astype(jnp.float32)[:, None] * freqs[None, :]
    return (jnp.cos(angles), jnp.sin(angles))


def rotate(values, cosine, sine):
    half = values.shape[-1] // 2
    first = values[..., :half]
    second = values[..., half:]
    cosine = cosine[:, None, :]
    sine = sine[:, None, :]
    return jnp.concatenate(
        [first * cosine - second * sine, second * cosine + first * sine], axis=-1
    )


def rotate_back(grads, cosine, sine):
    half = grads.shape[-1] // 2
    first = grads[..., :half]
    second = grads[..., half:]
    cosine = cosine[:, None, :]
    sine = sine[:, None, :]
    return jnp.concatenate(
        [first * cosine + second * sine, second * cosine - first * sine], axis=-1
    )


def inverse(order, count):
    slots = jnp.arange(count, dtype=jnp.int32)
    matches = order[None, :] == slots[:, None]
    return jnp.sum(jnp.where(matches, slots[None, :], 0), axis=1)


def dot(left, right):
    return lax.dot_general(
        left, right, (((1,), (0,)), ((), ())), preferred_element_type=jnp.float32
    )


def dot_nt(left, right):
    return lax.dot_general(
        left, right, (((1,), (1,)), ((), ())), preferred_element_type=jnp.float32
    )


def dot_tn(left, right):
    return lax.dot_general(
        left, right, (((0,), (0,)), ((), ())), preferred_element_type=jnp.float32
    )


def swap(block):
    return lax.ppermute(block, "mp", [(0, 1), (1, 0)])


def cycle(block, axis, distance):
    count = lax.axis_size(axis)
    return lax.ppermute(block, axis, [(i, (i + distance) % count) for i in range(count)])


def tie(value, *others):
    return lax.optimization_barrier((value,) + others)[0]


def pick(blocks, index):
    return lax.dynamic_index_in_dim(blocks, index, 0, keepdims=False, allow_negative_indices=False)


def wrap(index, count):
    return index & (count - 1) if count & (count - 1) == 0 else lax.rem(index, count)


def gather_ctx(block):
    blocks = [block]
    for _ in range(lax.axis_size("ctx") - 1):
        blocks.append(cycle(blocks[-1], "ctx", 1))
    return blocks


def scatter_ctx(parts, steps=None):
    total = parts[1]
    for part in parts[2:] + parts[:1]:
        sent = total.astype(jnp.bfloat16)
        if steps is not None:
            steps.append(sent)
        arrived = cycle(sent, "ctx", 1)
        total = arrived.astype(jnp.float32) + part
    return total


def gather_ctx_direct(block):
    return [block] + [cycle(block, "ctx", s) for s in range(1, lax.axis_size("ctx"))]


def scatter_ctx_direct(parts):
    total = parts[0]
    for s in range(1, len(parts)):
        arrived = cycle(parts[s].astype(jnp.bfloat16), "ctx", -s)
        total = total + arrived.astype(jnp.float32)
    return total


def neighbour(block, bit):
    return lax.ppermute(block, "dp", [(i, i ^ bit) for i in range(4)])


def gather_dp(block):
    count = lax.axis_size("dp")
    rows, cols = block.shape
    if count != 4:
        return lax.all_gather(block, "dp", axis=0, tiled=True)
    half = rows // 2
    index = lax.axis_index("dp")
    along_x = neighbour(block, 1)
    along_y = neighbour(block, 2)
    far_first = neighbour(along_x[:half], 2)
    far_second = neighbour(along_y[half:], 1)
    whole = jnp.zeros((count, rows, cols), block.dtype)

    def place(whole, part, where, start):
        return lax.dynamic_update_slice(
            whole, part[None], (where, 0 * where + start, 0 * where), allow_negative_indices=False
        )

    whole = place(whole, block, index, 0)
    whole = place(whole, along_x, index ^ 1, 0)
    whole = place(whole, along_y, index ^ 2, 0)
    whole = place(whole, far_first, index ^ 3, 0)
    whole = place(whole, far_second, index ^ 3, half)
    return whole.reshape(count * rows, cols)


def scatter_dp(terms, *others):
    count = lax.axis_size("dp")
    rows, cols = terms.shape[0] // count, terms.shape[1]
    if count != 4:
        return lax.psum_scatter(terms, "dp", scatter_dimension=0, tiled=True).astype(jnp.float32)
    half = rows // 2
    index = lax.axis_index("dp")
    terms = terms.reshape(count, rows, cols)
    wide = lambda value: value.astype(jnp.float32)
    far = pick(terms, index ^ 3)
    from_x = neighbour(far[:half], 1)
    from_y = neighbour(far[half:], 2)
    to_x = wide(pick(terms, index ^ 1))
    to_y = wide(pick(terms, index ^ 2))
    if others:
        from_y = tie(from_y, *others)
        from_x = tie(from_x, *others)
    to_x = jnp.concatenate([to_x[:half], to_x[half:] + wide(from_y)]).astype(jnp.bfloat16)
    to_y = jnp.concatenate([to_y[:half] + wide(from_x), to_y[half:]]).astype(jnp.bfloat16)
    return wide(pick(terms, index)) + wide(neighbour(to_x, 1)) + wide(neighbour(to_y, 2))


def sum_all(block):
    block = block + swap(block)
    for axis in ("ctx", "dp"):
        count = lax.axis_size(axis)
        terms = jnp.stack([block] + [cycle(block, axis, s) for s in range(1, count)])
        index = lax.axis_index(axis)
        block = sum(pick(terms, wrap(index + count - j, count)) for j in range(count))
    return block


GROUPS = 3


def combine(weights, blocks):
    return sum(weights[k] * blocks[k].astype(jnp.float32) for k in range(len(blocks)))


def fold(block):
    tall = block.shape[0] // GROUPS
    return jnp.concatenate([block[g * tall : (g + 1) * tall] for g in range(GROUPS)], axis=1)


def unfold(block):
    wide = block.shape[1] // GROUPS
    return jnp.concatenate([block[:, g * wide : (g + 1) * wide] for g in range(GROUPS)], axis=0)


ATTEND_ROWS = 512


def seen_part(queries, keys, query_code, key_code, number):
    start = number * ATTEND_ROWS
    span = slice(start, start + ATTEND_ROWS + WINDOW)
    here = slice(start, start + ATTEND_ROWS)
    raw = dot_nt(queries[here], keys[span]) * HEAD_SIZE ** (-0.5)
    bent = jnp.tanh(raw * (1.0 / soft_cap))
    row = lax.broadcasted_iota(jnp.int32, raw.shape, 0)
    col = lax.broadcasted_iota(jnp.int32, raw.shape, 1)
    visible = (query_code[here] == key_code[:, span]) & (col > row) & (col <= row + WINDOW)
    visible = visible | (col == row + WINDOW)
    return here, span, jnp.where(visible, jnp.exp(soft_cap * bent), 0.0), bent


def attend_forward(queries, both, prev_both, query_code, key_code):
    joined = jnp.concatenate([prev_both, both], axis=0)
    keys, values = joined[:, :HEAD_SIZE], joined[:, HEAD_SIZE:]
    outs, sums = [], []
    for number in range(queries.shape[0] // ATTEND_ROWS):
        _, span, expo, _ = seen_part(queries, keys, query_code, key_code, number)
        total = jnp.sum(expo, axis=1, keepdims=True)
        outs.append(dot(expo.astype(jnp.bfloat16), values[span]) / total)
        sums.append(total)
    out = jnp.concatenate(outs, axis=0)
    return out.astype(jnp.bfloat16), out, jnp.concatenate(sums, axis=0)


def attend_backward(queries, both, prev_both, query_code, key_code, grads, full, sums):
    rows = queries.shape[0]
    scale = HEAD_SIZE ** (-0.5)
    joined = jnp.concatenate([prev_both, both], axis=0)
    keys, values = joined[:, :HEAD_SIZE], joined[:, HEAD_SIZE:]
    query_grads, pieces = [], []
    for number in range(rows // ATTEND_ROWS):
        here, span, expo, bent = seen_part(queries, keys, query_code, key_code, number)
        probs = expo * (1.0 / sums[here])
        prob_grad = dot_nt(grads[here], values[span])
        delta = jnp.sum(grads[here].astype(jnp.float32) * full[here], axis=1, keepdims=True)
        score = (probs * (prob_grad - delta) * (1.0 - bent * bent)).astype(jnp.bfloat16)
        query_grads.append(dot(score, keys[span]) * scale)
        part = jnp.concatenate(
            [dot_tn(score, queries[here]) * scale, dot_tn(probs.astype(jnp.bfloat16), grads[here])],
            axis=1,
        )
        pieces.append(jnp.pad(part, ((span.start, 2 * rows - span.stop), (0, 0))))
    total = sum(pieces)
    return (
        jnp.concatenate(query_grads, axis=0),
        total[rows:],
        total[:rows].astype(jnp.bfloat16),
    )


def body(
    tokens,
    cotangent,
    segments,
    padding,
    owners,
    gains,
    gain_stats,
    attention_input_master,
    attn_out,
    mlp_in,
    mlp_out,
    left_stats,
    right_stats,
    left_roots,
    right_roots,
):
    nctx = lax.axis_size("ctx")
    ctx_index = lax.axis_index("ctx")
    dp_index = lax.axis_index("dp")
    mp_index = lax.axis_index("mp")
    rows, width = tokens.shape
    half = rows // 2
    group_rows = rows * nctx
    dblock = attention_input_master.shape[0]
    key_columns = (attention_input_master.shape[1] - HEAD_SIZE) // 2
    ffn_cols = mlp_out.shape[1]
    piece = ffn_cols // nctx
    per_head = HEAD_SIZE // key_columns
    head_group = QUERY_HEADS // KEY_VALUE_HEADS
    before = lambda s: wrap(ctx_index + nctx - s, nctx)
    slots = jnp.arange(nctx, dtype=jnp.int32)
    one = lambda condition: condition.astype(jnp.float32)
    held = one(owners[:, None, :] == slots[None, :, None])
    turned_to = one(slots[None, :] == ((ctx_index + nctx - slots) % nctx)[:, None])
    my_query = jnp.sum(held[0] * turned_to[0][None, :], axis=1)
    key_weights, value_weights = [], []
    for part in range(per_head):
        wanted = one(slots[:, None] == (slots // head_group * per_head + part)[None, :])
        column = jnp.sum(wanted * my_query[None, :], axis=1)
        for row, weights in ((1, key_weights), (2, value_weights)):
            holder = jnp.sum(held[row] * column[:, None], axis=0)
            weights.append(jnp.sum(turned_to * holder[None, :], axis=1))
    paired = jnp.sum(held[0][:, :, None] * held[3][:, None, :], axis=0)
    paired_back = jnp.sum(paired[:, None, :] * turned_to[None, :, :], axis=2)

    def halves(block):
        pair = block.reshape((2, block.shape[0] // 2) + block.shape[1:])
        return jnp.where(mp_index == 0, pair, pair[::-1]).reshape(block.shape)

    def own_half(block):
        return lax.dynamic_slice_in_dim(block, mp_index * half, half, 0, allow_negative_indices=False)

    def other_half(block):
        return lax.dynamic_slice_in_dim(
            block, (1 - mp_index) * half, half, 0, allow_negative_indices=False
        )

    def both(block):
        return jnp.concatenate([block, swap(block)], axis=0)

    def in_order(blocks):
        stacked = jnp.stack(blocks)
        return jnp.concatenate([pick(stacked, before(j)) for j in range(nctx)], axis=0)

    def reduce_width(parts, steps=None):
        terms = []
        for part in parts:
            arrived = swap(part[half:].astype(jnp.bfloat16)).astype(jnp.float32)
            terms.append(part[:half] + arrived)
        return scatter_ctx(terms, steps)

    key_value = gather_ctx_direct(attention_input_master[:, HEAD_SIZE:].astype(jnp.bfloat16))
    low_in = [attention_input_master[:, :HEAD_SIZE]]
    for start, table in ((0, key_weights), (key_columns, value_weights)):
        parts = [block[:, start : start + key_columns] for block in key_value]
        low_in += [combine(weights, parts) for weights in table]
    whole_in = gather_dp(jnp.concatenate(low_in, axis=1).astype(jnp.bfloat16))

    def pass_on(block):
        return lax.all_to_all(block, "ctx", split_axis=0, concat_axis=0, tiled=True)

    def quarters_of(block):
        return [block[:, k * piece : (k + 1) * piece] for k in range(nctx)]

    def spread(master, column, row, *others):
        block = master if column is None else master[:, column[0] : column[0] + column[1]]
        dealt = jnp.stack([fold(quarter) for quarter in quarters_of(block.astype(jnp.bfloat16))])
        came = pass_on(tie(dealt, *others))
        blocks = [
            unfold(combine(held[row][b], [came[k] for k in range(nctx)]).astype(jnp.bfloat16))
            for b in range(nctx)
        ]
        return came, jnp.concatenate(blocks, axis=1)

    gate_came, low_gate = spread(mlp_in, (0, ffn_cols), 4, *key_value[1:])
    whole_gate = gather_dp(low_gate)
    out_blocks = gather_ctx_direct(tie(attn_out.astype(jnp.bfloat16), gate_came))
    whole_out = gather_dp(
        jnp.concatenate([combine(paired_back[j], out_blocks) for j in range(nctx)], axis=1).astype(
            jnp.bfloat16
        )
    )

    inputs = own_half(tokens).astype(jnp.float32)
    first_out, first_normed, first_scale = normalize(inputs, gains[0])
    first_blocks = gather_ctx(tie(first_out.astype(jnp.bfloat16), out_blocks[2]))
    hidden_in = [both(block) for block in first_blocks]
    _, low_up = spread(mlp_in, (ffn_cols, ffn_cols), 5, first_blocks[3])
    whole_up = gather_dp(low_up)
    _, low_down = spread(mlp_out, None, 6, first_blocks[3])
    whole_down = gather_dp(low_down)
    projected = in_order([halves(dot(block, whole_in)) for block in hidden_in])
    group_first = dp_index * group_rows
    group_pos = group_first + jnp.arange(group_rows, dtype=jnp.int32)
    cosine, sine = rotation(group_pos % PACKED_TOKENS)
    turned = rotate(
        projected[:, : 2 * HEAD_SIZE].reshape(group_rows, 2, HEAD_SIZE), cosine, sine
    ).astype(jnp.bfloat16)
    queries_h = turned[:, 0]
    both_h = jnp.concatenate(
        [turned[:, 1], projected[:, 2 * HEAD_SIZE :].astype(jnp.bfloat16)], axis=1
    )
    prev_both = shifted(both_h, "dp", 1)
    codes = segments + PACKED_TOKENS * (
        jnp.arange(segments.shape[0], dtype=jnp.int32) // PACKED_TOKENS
    )
    nobody = jnp.full((group_rows,), -1, jnp.int32)
    key_codes = jnp.concatenate([nobody, jnp.where(padding == 1, codes, -1)])
    key_code = lax.dynamic_slice_in_dim(
        key_codes, group_first, 2 * group_rows, 0, allow_negative_indices=False
    )[None, :]
    query_code = lax.dynamic_slice_in_dim(
        codes, group_first, group_rows, 0, allow_negative_indices=False
    )[:, None]
    attended_low, attended, prob_sums = attend_forward(
        tie(queries_h, low_up), both_h, prev_both, query_code, key_code
    )
    came = pass_on(attended_low.reshape(nctx, rows, HEAD_SIZE))
    heads_out = jnp.concatenate([came[j] for j in range(nctx)], axis=1)
    attn_part = dot_nt(tie(heads_out, low_down), whole_out)
    attn = own_half(attn_part) + swap(other_half(attn_part).astype(jnp.bfloat16)).astype(
        jnp.float32
    )
    second_out, second_normed, second_scale = normalize(attn, gains[1])
    mixed = inputs + second_out
    third_out, third_normed, third_scale = normalize(mixed, gains[2])

    hidden_two = [both(block) for block in gather_ctx(third_out.astype(jnp.bfloat16))]
    pulls, actives, uppers, gelus, moved_parts = [], [], [], [], []
    for block in hidden_two:
        gate = dot(block, whole_gate)
        upper = dot(block, whole_up)
        gelu_value, gelu_pull = jax.vjp(lambda values: jax.nn.gelu(values, approximate=True), gate)
        active = (gelu_value * upper).astype(jnp.bfloat16)
        pulls.append(gelu_pull)
        actives.append(active)
        uppers.append(upper)
        gelus.append(gelu_value)
        moved_parts.append(dot_nt(active, whole_down))
    moved = reduce_width(moved_parts)
    fourth_out, fourth_normed, fourth_scale = normalize(moved, gains[3])
    block_out = halves(both((mixed + fourth_out).astype(jnp.bfloat16)))
    upstream = own_half(cotangent).astype(jnp.float32)
    moved_grad, fourth_gain = norm_back(fourth_normed, fourth_scale, gains[3], upstream)
    moved_low = [both(block) for block in gather_ctx(moved_grad.astype(jnp.bfloat16))]
    gate_grads, upper_grads, hidden_two_parts = [], [], []
    for s, block in enumerate(moved_low):
        active_grad = dot(block, whole_down)
        gate_grad = pulls[s](active_grad * uppers[s])[0].astype(jnp.bfloat16)
        upper_grad = (active_grad * gelus[s]).astype(jnp.bfloat16)
        gate_grads.append(gate_grad)
        upper_grads.append(upper_grad)
        hidden_two_parts.append(dot_nt(gate_grad, whole_gate) + dot_nt(upper_grad, whole_up))
    steps = []
    hidden_two_grad = reduce_width(hidden_two_parts, steps)
    cat = lambda values: jnp.concatenate(values, axis=0)
    low = lambda values: values.astype(jnp.bfloat16)
    down_terms = low(dot_tn(cat(moved_low), cat(actives)))
    hidden_two_all = cat(hidden_two)
    gate_terms = low(dot_tn(hidden_two_all, tie(cat(gate_grads), steps[1])))
    up_terms = low(dot_tn(hidden_two_all, tie(cat(upper_grads), steps[2])))
    down_sum = scatter_dp(down_terms)
    gate_sum = scatter_dp(gate_terms)

    def collect(summed, row):
        quarters = quarters_of(summed)
        dealt = [fold(low(combine(held[row][:, k], quarters))) for k in range(nctx)]
        came = pass_on(jnp.stack(dealt))
        return came, jnp.concatenate([unfold(came[j]) for j in range(nctx)], axis=1).astype(
            jnp.float32
        )

    mixed_part, third_gain = norm_back(third_normed, third_scale, gains[2], hidden_two_grad)
    mixed_grad = upstream + mixed_part
    attn_grad, second_gain = norm_back(second_normed, second_scale, gains[1], mixed_grad)
    attn_low = halves(both(attn_grad.astype(jnp.bfloat16)))
    heads_grad = low(dot(attn_low, whole_out))

    head_grad = pass_on(
        jnp.stack([heads_grad[:, j * HEAD_SIZE : (j + 1) * HEAD_SIZE] for j in range(nctx)])
    ).reshape(group_rows, HEAD_SIZE)

    query_grads, both_own, both_prev = attend_backward(
        queries_h, both_h, prev_both, query_code, key_code, head_grad, attended, prob_sums
    )
    both_next = shifted(both_prev, "dp", -1)
    up_sum = scatter_dp(up_terms, both_next)
    down_came, down_grad = collect(tie(down_sum, head_grad), 6)
    gate_came, gate_grad_whole = collect(tie(gate_sum, down_came), 4)
    up_came, up_grad_whole = collect(tie(up_sum, gate_came), 5)
    both_total = both_own + both_next.astype(jnp.float32)
    turned_back = rotate_back(
        jnp.stack([query_grads, both_total[:, :HEAD_SIZE]], axis=1), cosine, sine
    ).reshape(group_rows, 2 * HEAD_SIZE)
    right_attn = low(jnp.concatenate([turned_back, both_total[:, HEAD_SIZE:]], axis=1)).reshape(
        nctx, rows, 3 * HEAD_SIZE
    )
    right_attn = cat([halves(pick(right_attn, before(s))) for s in range(nctx)])
    parts = [dot_nt(right_attn[s * rows : (s + 1) * rows], whole_in) for s in range(nctx)]
    terms = [part[:half] + swap(low(part[half:])).astype(jnp.float32) for part in parts]
    sent_one = low(terms[1])
    sent_two = low(cycle(sent_one, "ctx", 1).astype(jnp.float32) + terms[2])
    sent_two = tie(sent_two, gate_came)
    sent_three = low(cycle(sent_two, "ctx", 1).astype(jnp.float32) + terms[3])
    hidden_grad = cycle(sent_three, "ctx", 1).astype(jnp.float32) + terms[0]
    input_part, first_gain = norm_back(first_normed, first_scale, gains[0], hidden_grad)
    input_grad = halves(both(mixed_grad + input_part))

    out_sum = scatter_dp(low(dot_tn(tie(attn_low, sent_one), heads_out)))
    in_terms = low(dot_tn(cat(hidden_in), tie(right_attn, sent_one)))
    in_sum = scatter_dp(in_terms)
    heads = [out_sum[:, j * HEAD_SIZE : (j + 1) * HEAD_SIZE] for j in range(nctx)]
    heads[0] = tie(heads[0], up_came)
    out_grad = scatter_ctx_direct([combine(paired_back[:, s], heads) for s in range(nctx)])
    sums = [
        in_sum[:, start + p * key_columns : start + (p + 1) * key_columns]
        for start in (HEAD_SIZE, 2 * HEAD_SIZE)
        for p in range(per_head)
    ]
    key_value_grad = scatter_ctx_direct(
        [
            jnp.concatenate(
                [
                    sum(weights[s] * block for weights, block in zip(table, blocks))
                    for table, blocks in (
                        (key_weights, sums[:per_head]),
                        (value_weights, sums[per_head:]),
                    )
                ],
                axis=1,
            )
            for s in range(nctx)
        ]
    )
    grad_attn_in = jnp.concatenate([in_sum[:, :HEAD_SIZE], key_value_grad], axis=1)
    grad_mlp_in = jnp.concatenate([gate_grad_whole, up_grad_whole], axis=1)

    gain_grad = sum_all(jnp.stack([first_gain, second_gain, third_gain, fourth_gain], axis=0))
    new_gain_stats = stat_decay * gain_stats + (1.0 - stat_decay) * gain_grad * gain_grad
    new_gains = gains - gain_rate * gain_grad * lax.rsqrt(new_gain_stats)

    stats = tuple(
        value.reshape(value.shape[3:])
        for value in (left_stats, right_stats, left_roots, right_roots)
    )
    in_blocks = attention_input_master.shape[1] // SUBW
    ffn_blocks = ffn_cols // SUBW
    first = in_blocks + attn_out.shape[1] // SUBW
    batched = lambda left, right, sum_left, sum_right: lax.dot_general(
        left, right, (((sum_left,), (sum_right,)), ((0,), (0,))), preferred_element_type=jnp.float32
    )

    def blocks_of(grad):
        split = grad.reshape(dblock, grad.shape[1] // SUBW, SUBW)
        return jnp.transpose(low(split), (1, 0, 2))

    def renew(master, blocks, start):
        span = slice(start, start + blocks.shape[0])
        step = batched(low(batched(low(stats[2][span]), blocks, 2, 1)), low(stats[3][span]), 2, 1)
        return master - master_rate * jnp.transpose(step, (1, 0, 2)).reshape(master.shape)

    down_blocks = blocks_of(down_grad)
    new_mlp_out = renew(mlp_out, down_blocks, first + 2 * ffn_blocks)
    gate_blocks = blocks_of(gate_grad_whole)
    up_blocks = blocks_of(up_grad_whole)
    new_mlp_in = jnp.concatenate(
        [
            renew(mlp_in[:, :ffn_cols], gate_blocks, first),
            renew(mlp_in[:, ffn_cols:], up_blocks, first + ffn_blocks),
        ],
        axis=1,
    )
    pieces = [blocks_of(grad) for grad in (grad_attn_in, out_grad)]
    stacked = jnp.concatenate(pieces + [gate_blocks, up_blocks, down_blocks], axis=0)
    new_left = stat_decay * stats[0] + (1.0 - stat_decay) * batched(stacked, stacked, 2, 2)
    new_right = stat_decay * stats[1] + (1.0 - stat_decay) * batched(stacked, stacked, 1, 1)
    new_attn_in = renew(attention_input_master, pieces[0], 0)
    new_attn_out = renew(attn_out, pieces[1], in_blocks)
    return (
        block_out,
        input_grad,
        grad_attn_in,
        out_grad,
        grad_mlp_in,
        down_grad,
        new_attn_in,
        new_attn_out,
        new_mlp_in,
        new_mlp_out,
        new_left.reshape(left_stats.shape),
        new_right.reshape(right_stats.shape),
        gain_grad,
        new_gain_stats,
        new_gains,
    )


def solution(mesh):
    return jax.shard_map(
        body,
        mesh=mesh,
        in_specs=(
            P(("dp", "ctx"), None),
            P(("dp", "ctx"), None),
            P(),
            P(),
            P(),
            P(),
            P(),
            P("dp", ("ctx", "mp")),
            P("dp", ("ctx", "mp")),
            P("dp", ("ctx", "mp")),
            P("dp", ("ctx", "mp")),
            P("dp", "ctx", "mp", None, None, None),
            P("dp", "ctx", "mp", None, None, None),
            P("dp", "ctx", "mp", None, None, None),
            P("dp", "ctx", "mp", None, None, None),
        ),
        out_specs=(
            P(("dp", "ctx"), None),
            P(("dp", "ctx"), None),
            P("dp", ("ctx", "mp")),
            P("dp", ("ctx", "mp")),
            P("dp", ("ctx", "mp")),
            P("dp", ("ctx", "mp")),
            P("dp", ("ctx", "mp")),
            P("dp", ("ctx", "mp")),
            P("dp", ("ctx", "mp")),
            P("dp", ("ctx", "mp")),
            P("dp", "ctx", "mp", None, None, None),
            P("dp", "ctx", "mp", None, None, None),
            P(),
            P(),
            P(),
        ),
        check_vma=False,
    )
```
